256 devices in a mesh: row: 4 (over x), col: 16 (over z, core), depth: 4 (over y).
Axes of the slice: x: 4, y: 4, z: 8, core: 2. Of those that a mesh axis runs over, the one named last changes fastest.
Arguments:
- tokens: bfloat16 [1024, 8192], P('row', 'col'), may hold values from -6 to 6
- gate_weight: bfloat16 [8192, 14336], P('col', ('row', 'depth')), may hold values from -0.0625 to 0.0625
- up_weight: bfloat16 [8192, 14336], P('col', ('row', 'depth')), may hold values from -0.0625 to 0.0625
- down_weight: bfloat16 [14336, 8192], P(('row', 'depth'), 'col'), may hold values from -0.046875 to 0.046875
- grad_out: bfloat16 [1024, 8192], P('row', 'col'), may hold values from -3 to 3
Outputs:
- mixed: bfloat16 [1024, 8192], P('row', 'col')
- grad_tokens: bfloat16 [1024, 8192], P('row', 'col')
- grad_gate: bfloat16 [8192, 14336], P('col', ('row', 'depth'))
- grad_up: bfloat16 [8192, 14336], P('col', ('row', 'depth'))
- grad_down: bfloat16 [14336, 8192], P(('row', 'depth'), 'col')
The draws below stay inside these ranges and needn't reach their ends.
All inputs are finite; a program needn't handle non-finite values.
Results may differ from the reference program's by a relative error of at most 0.005.
Values may be sent and summed in bfloat16 or wider, within the bound.
No kernel may reach another device: no remote copies, remote signals or barrier semaphores. Data moves between devices by JAX's collectives and lax.ppermute only.
A program may use at most 128 MiB of HBM per device.

```python
import jax
import jax.numpy as jnp

D = 8192
FF = 14336
TOKENS = 1024


def shard_levels(rng, dims, split, least, high):
    level = 1.0
    for dim, shards_of in split:
        steps = jax.random.uniform(jax.random.fold_in(jax.random.fold_in(rng, 6), dim), (shards_of,), jnp.float32, least / len(split), high / len(split))
        level = level * jnp.repeat(jnp.exp(steps), dims[dim] // shards_of).reshape((-1,) + (1,) * (len(dims) - 1 - dim))
    return level


def gaussian(own_key, shape, spread, limit, cuts=(), dtype=jnp.bfloat16):
    factor_of = shard_levels(own_key, shape, cuts, -0.22, 0.18) if cuts else 1.0
    array = jax.random.normal(own_key, shape, jnp.float32) * spread * factor_of
    return jnp.minimum(jnp.maximum(array, -limit), limit).astype(dtype)


def setup_inputs(seed: int = 0) -> dict:
    key_list = jax.random.split(jax.random.key(seed), 6)
    return {
        "tokens": gaussian(key_list[0], (TOKENS, D), 1.0, 6.0, ((0, 4), (1, 16))),
        "gate_weight": gaussian(key_list[1], (D, FF), D ** -0.5, 0.0625, ((0, 16), (1, 16))),
        "up_weight": gaussian(key_list[2], (D, FF), D ** -0.5, 0.0625, ((0, 16), (1, 16))),
        "down_weight": gaussian(key_list[3], (FF, D), FF ** -0.5, 0.046875, ((0, 16), (1, 16))),
        "grad_out": gaussian(key_list[4], (TOKENS, D), 0.5, 3.0, ((0, 4), (1, 16))),
    }


def reference(tokens, gate_weight, up_weight, down_weight, grad_out):
    gate = jnp.dot(tokens, gate_weight, preferred_element_type=jnp.float32)
    up = jnp.dot(tokens, up_weight, preferred_element_type=jnp.float32)
    sig = jax.nn.sigmoid(gate)
    hidden = (gate * sig * up).astype(jnp.bfloat16)
    mixed = jnp.dot(hidden, down_weight, preferred_element_type=jnp.float32).astype(jnp.bfloat16)
    grad_hidden = jnp.dot(grad_out, down_weight.T, preferred_element_type=jnp.float32)
    grad_gate_act = (grad_hidden * up * sig * (1.0 + gate * (1.0 - sig))).astype(jnp.bfloat16)
    grad_up_act = (grad_hidden * gate * sig).astype(jnp.bfloat16)
    grad_tokens = (jnp.dot(grad_gate_act, gate_weight.T, preferred_element_type=jnp.float32)
                   + jnp.dot(grad_up_act, up_weight.T, preferred_element_type=jnp.float32)).astype(jnp.bfloat16)
    grad_gate = jnp.dot(tokens.T, grad_gate_act, preferred_element_type=jnp.float32).astype(jnp.bfloat16)
    grad_up = jnp.dot(tokens.T, grad_up_act, preferred_element_type=jnp.float32).astype(jnp.bfloat16)
    grad_down = jnp.dot(hidden.T, grad_out, preferred_element_type=jnp.float32).astype(jnp.bfloat16)
    return mixed, grad_tokens, grad_gate, grad_up, grad_down
```

```python
import jax
import jax.numpy as jnp
from jax import lax
from jax.sharding import PartitionSpec as P

BF = jnp.bfloat16
F32 = jnp.float32
WIRE = jnp.float16
SUM_SCALE = 16.0


def dot(left, right, dims):
    return lax.dot_general(left, right, ((dims[:1], dims[1:]), ((), ())), preferred_element_type=F32)


def per_device(tokens, gate_weight, up_weight, down_weight, grad_out):
    rows, width = tokens.shape
    hidden_width = gate_weight.shape[1]
    n_col = lax.axis_size("col")
    n_row = lax.axis_size("row")
    n_depth = lax.axis_size("depth")
    n_z = n_col // 2
    col = lax.axis_index("col")
    z = col // 2
    core = col % 2
    half = rows // 2
    piece = half // n_z

    def swap(x):
        return lax.ppermute(x, "col", [(i, i ^ 1) for i in range(n_col)])

    def to_z(x, k):
        return lax.ppermute(x, "col", [(i, (i + 2 * k) % n_col) for i in range(n_col)])

    def to_row(x, k):
        return lax.ppermute(x, "row", [(i, (i + k) % n_row) for i in range(n_row)])

    def to_depth(x, k):
        return lax.ppermute(x, "depth", [(i, (i + k) % n_depth) for i in range(n_depth)])

    gate_sib, up_sib, down_sib = swap(gate_weight), swap(up_weight), swap(down_weight)
    both = jnp.concatenate([gate_weight, up_weight], axis=1)
    both_sib = jnp.concatenate([gate_sib, up_sib], axis=1)

    def halves(x):
        x = x.reshape(2, n_z, piece, -1)
        x = jnp.roll(x, (-core, -z), (0, 1))
        return x[0], x[1]

    own = (tokens, grad_out)
    left = tuple(to_row(x, 1) for x in own)
    right = tuple(to_row(x, -1) for x in own)
    far = tuple(
        jnp.concatenate([to_row(a[:half], 1), to_row(b[half:], -1)], axis=0)
        for a, b in zip(left, right)
    )
    blocks = [own, left, right, far]
    units = [[0], [1, 2], [3]]

    mine, other = [], []
    for t, g in blocks:
        (t0, t1), (g0, g1) = halves(t), halves(g)
        mine.append((t0, g0))
        other.append((t1, g1))

    def cat(parts):
        return parts[0] if len(parts) == 1 else jnp.concatenate(parts, axis=1)

    cut = (3 * hidden_width // 256 + 1) * 128
    all_tokens, all_grads, all_acts, sums = [], [], [], []
    for unit in units:
        t_mine = cat([mine[b][0] for b in unit])
        g_mine = cat([mine[b][1] for b in unit])
        t_other = cat([other[b][0] for b in unit])
        g_other = cat([other[b][1] for b in unit])
        n = t_mine.shape[1]
        t_sib, g_sib = swap(t_other), swap(g_other)
        flat = lambda x: x.reshape(-1, x.shape[-1])
        gu = dot(flat(t_mine), both, (1, 0)) + dot(flat(t_sib), both_sib, (1, 0))
        gh = dot(flat(g_mine), down_weight, (1, 1)) + dot(flat(g_sib), down_sib, (1, 1))
        part = (jnp.concatenate([gu, gh], axis=1) * SUM_SCALE).reshape(n_z, n, -1)

        plus = to_z(part[4][:, :cut].astype(WIRE), 1)
        minus = to_z(part[4][:, cut:].astype(WIRE), -1)
        plus = jnp.pad(plus.astype(F32), ((0, 0), (0, part.shape[2] - cut)))
        minus = jnp.pad(minus.astype(F32), ((0, 0), (cut, 0)))
        for k in (3, 2, 1):
            plus = to_z((part[k] + plus).astype(WIRE), 1).astype(F32)
            minus = to_z((part[n_z - k] + minus).astype(WIRE), -1).astype(F32)
        total = (part[0] + plus + minus) * (1.0 / SUM_SCALE)
        gate, up, grad_hidden = (total[:, i * hidden_width : (i + 1) * hidden_width] for i in range(3))
        sig = jax.nn.sigmoid(gate)
        act = jnp.concatenate(
            [
                (gate * sig * up).astype(BF),
                (grad_hidden * up * sig * (1.0 + gate * (1.0 - sig))).astype(BF),
                (grad_hidden * gate * sig).astype(BF),
            ],
            axis=1,
        )

        got = {0: act}
        up_way, down_way = act, act
        for k in (1, 2, 3):
            up_way, down_way = to_z(up_way, 1), to_z(down_way, -1)
            got[n_z - k], got[k] = up_way, down_way
        got[4] = jnp.concatenate(
            [to_z(up_way[:, :cut], 1), to_z(down_way[:, cut:], -1)], axis=1
        )
        act = jnp.concatenate([got[k] for k in range(n_z)], axis=0)
        act = jnp.concatenate([act, swap(act)], axis=0)
        all_acts.append(act)
        all_tokens += [flat(t_mine), flat(t_other)]
        all_grads += [flat(g_mine), flat(g_other)]
        mixed = dot(act[:, :hidden_width], down_weight, (1, 0))
        back = dot(act[:, hidden_width:], both, (1, 1))
        out = jnp.concatenate([mixed, back], axis=1).reshape(2, n_z, len(unit), piece, -1)
        for i in range(len(unit)):
            sums.append(out[:, :, i].reshape(rows, -1))

    own_s, left_s, right_s, far_s = sums
    h1 = to_row(far_s[:half].astype(BF), 1).astype(F32)
    h2 = to_row(far_s[half:].astype(BF), -1).astype(F32)
    to_right = jnp.concatenate([right_s[:half] + h1, right_s[half:]], axis=0)
    to_left = jnp.concatenate([left_s[:half], left_s[half:] + h2], axis=0)
    total = own_s + to_row(to_right.astype(BF), 1).astype(F32) + to_row(to_left.astype(BF), -1).astype(F32)
    quarter = rows // n_depth
    d = lax.axis_index("depth")
    total = jnp.roll(total.reshape(n_depth, quarter, -1), -d, 0)
    got = [to_depth(total[k].astype(BF), k) for k in range(1, n_depth)]
    done = total[0]
    for x in got:
        done = done + x.astype(F32)
    done = done.astype(BF)
    final = jnp.stack([done] + [to_depth(done, -k) for k in range(1, n_depth)])
    final = jnp.roll(final, d, 0).reshape(2, n_z, piece, -1)
    final = jnp.roll(final, (core, z), (0, 1)).reshape(rows, -1)
    mixed, grad_tokens = final[:, :width], final[:, width:]

    acts = jnp.concatenate(all_acts, axis=0)
    toks = jnp.concatenate(all_tokens, axis=0)
    grads = jnp.concatenate(all_grads, axis=0)
    grad_down = dot(acts[:, :hidden_width], grads, (0, 0)).astype(BF)
    grad_gate = dot(toks, acts[:, hidden_width : 2 * hidden_width], (0, 0)).astype(BF)
    grad_up = dot(toks, acts[:, 2 * hidden_width :], (0, 0)).astype(BF)
    return (mixed, grad_tokens, grad_gate, grad_up, grad_down)


def solution(mesh):
    in_specs = (
        P("row", "col"),
        P("col", ("row", "depth")),
        P("col", ("row", "depth")),
        P(("row", "depth"), "col"),
        P("row", "col"),
    )
    out_specs = (
        P("row", "col"),
        P("row", "col"),
        P("col", ("row", "depth")),
        P("col", ("row", "depth")),
        P(("row", "depth"), "col"),
    )
    return jax.shard_map(
        per_device, mesh=mesh, in_specs=in_specs, out_specs=out_specs, check_vma=False
    )
```

```python
import jax
import jax.numpy as jnp
from jax import lax
from jax.experimental import pallas as pl
from jax.sharding import PartitionSpec as P

BF = jnp.bfloat16
F32 = jnp.float32
WIRE = jnp.float16
SUM_SCALE = 16.0


def dot(left, right, left_dim, right_dim):
    return lax.dot_general(
        left, right, (((left_dim,), (right_dim,)), ((), ())), preferred_element_type=F32
    )


def tie(*arrays):
    return lax.optimization_barrier(arrays)


def act_gradients(gate_up, grad_hidden, out):
    n = grad_hidden.shape[1]
    gate, up, grad = gate_up[:, :n], gate_up[:, n:], grad_hidden[...]
    sig = jax.nn.sigmoid(gate)
    out[:, :n] = (grad * up * sig * (1.0 + gate * (1.0 - sig))).astype(BF)
    out[:, n:] = (grad * gate * sig).astype(BF)


def per_device(tokens, gate_weight, up_weight, down_weight, grad_out):
    rows, width = tokens.shape
    hidden_width = gate_weight.shape[1]
    n_col = lax.axis_size("col")
    n_row = lax.axis_size("row")
    n_depth = lax.axis_size("depth")
    n_z = n_col // 2
    col = lax.axis_index("col")
    z = col // 2
    core = col % 2
    depth = lax.axis_index("depth")
    half = rows // 2
    piece = rows // n_col
    own_rows = n_row * piece
    far_z = n_z // 2

    def swap(x):
        return lax.ppermute(x, "col", [(i, i ^ 1) for i in range(n_col)])

    def to_z(x, k):
        return lax.ppermute(x, "col", [(i, (i + 2 * k) % n_col) for i in range(n_col)])

    def to_row(x, k):
        return lax.ppermute(x, "row", [(i, (i + k) % n_row) for i in range(n_row)])

    def to_depth(x, k):
        return lax.ppermute(x, "depth", [(i, (i + k) % n_depth) for i in range(n_depth)])

    def neighbours(x):
        return tie(to_row(x, 1), to_row(x, -1))

    def all_rows(x, before, after, far_low, far_high):
        far = jnp.concatenate([far_low, far_high], axis=0)
        blocks = [b.reshape(n_col, piece, width) for b in (x, before, after, far)]
        return jnp.concatenate(blocks, axis=1)

    def by_core(x):
        x = x.reshape((n_z, 2) + x.shape[1:])
        mine = lax.dynamic_index_in_dim(x, core, 1, keepdims=False)
        other = lax.dynamic_index_in_dim(x, 1 - core, 1, keepdims=False)
        return mine.reshape(-1, width), other.reshape(-1, width)

    t_before, t_after = neighbours(tokens)
    t_low, t_high, grad_out = tie(t_before[:half], t_after[half:], grad_out)
    t_low, t_high = to_row(t_low, 1), to_row(t_high, -1)
    g_before, g_after = neighbours(grad_out)
    both = jnp.concatenate([gate_weight, up_weight], axis=1)
    both_sib = jnp.concatenate([swap(gate_weight), swap(up_weight)], axis=1)
    all_tokens = all_rows(tokens, t_before, t_after, t_low, t_high)
    t_mine, t_other = by_core(all_tokens)
    t_sib = swap(t_other)
    gate_up = (dot(t_mine, both, 1, 0) + dot(t_sib, both_sib, 1, 0)) * SUM_SCALE
    g_before, g_after, _ = tie(g_before, g_after, t_sib)
    g_low, g_high = to_row(g_before[:half], 1), to_row(g_after[half:], -1)
    all_grads = all_rows(grad_out, g_before, g_after, g_low, g_high)
    g_mine, g_other = by_core(all_grads)
    g_sib = swap(g_other)
    down_sib = swap(down_weight)

    grad_hid = (dot(g_mine, down_weight, 1, 1) + dot(g_sib, down_sib, 1, 1)) * SUM_SCALE

    def ring_sum(parts, beside=()):
        n = parts.shape[1]
        parts = parts.reshape(n_z, own_rows, n)
        cut = (n // 256) * 128

        def part(k):
            return lax.dynamic_index_in_dim(parts, (z + k) % n_z, 0, keepdims=False)

        first = part(far_z).astype(WIRE)
        plus, minus = tie(first[:, :cut], first[:, cut:])
        plus, minus = tie(to_z(plus, 1), to_z(minus, -1))
        plus = jnp.pad(plus.astype(F32), ((0, 0), (0, n - cut)))
        minus = jnp.pad(minus.astype(F32), ((0, 0), (cut, 0)))
        for k in range(far_z - 1, 0, -1):
            plus, minus = (part(k) + plus).astype(WIRE), (part(n_z - k) + minus).astype(WIRE)
            plus, minus, *_ = tie(plus, minus, *(beside if k == 1 else ()))
            plus, minus = tie(to_z(plus, 1), to_z(minus, -1))
            plus, minus = plus.astype(F32), minus.astype(F32)
        return (part(0) + plus + minus) * (1.0 / SUM_SCALE)

    def both_ways(x):
        return tie(to_z(x, 1), to_z(x, -1))

    def gather(x, plus, minus):
        n = x.shape[1]
        cut = (n // 256) * 128
        out = jnp.zeros((n_z, own_rows, n), x.dtype)

        def put(out, x, k, at=0):
            return lax.dynamic_update_slice(out, x[None], ((z + k) % n_z, 0, at))

        out = put(out, x, 0)
        for k in range(1, far_z):
            if k > 1:
                plus, minus = tie(to_z(plus, 1), to_z(minus, -1))
            out = put(put(out, plus, n_z - k), minus, k)
        plus, minus = tie(to_z(plus[:, :cut], 1), to_z(minus[:, cut:], -1))
        out = put(put(out, plus, far_z), minus, far_z, cut)
        sib = swap(out)
        low, high = jnp.where(core == 0, out, sib), jnp.where(core == 0, sib, out)
        return jnp.stack([low, high], axis=1).reshape(-1, n)

    gate_up = ring_sum(gate_up)
    gate, up = gate_up[:, :hidden_width], gate_up[:, hidden_width:]
    hidden = (gate * jax.nn.sigmoid(gate) * up).astype(BF)
    hidden_next = both_ways(hidden)
    grad_hidden = ring_sum(grad_hid, hidden_next)
    hidden = gather(hidden, *hidden_next)
    act_grads = pl.pallas_call(
        act_gradients,
        out_shape=jax.ShapeDtypeStruct((own_rows, 2 * hidden_width), BF),
    )(gate_up, grad_hidden)
    act_grads = lax.all_gather(act_grads, "col", axis=0, tiled=True)

    mid = n_col // 2
    quarter = rows // n_depth

    def ring4(own, last, after, far, move):
        cut = far.shape[0] // 2
        low, high = tie(move(far[:cut], 1), move(far[cut:], -1))
        after = jnp.concatenate(
            [(after[:cut].astype(F32) + low.astype(F32)).astype(BF), after[cut:]], axis=0
        )
        last = jnp.concatenate(
            [last[:cut], (last[cut:].astype(F32) + high.astype(F32)).astype(BF)], axis=0
        )
        after, last = tie(after, last)
        low, high = tie(move(after, 1), move(last, -1))
        return own.astype(F32) + low.astype(F32) + high.astype(F32)

    mixed = dot(hidden, down_weight, 1, 0).astype(BF)
    mixed = mixed.reshape(n_col, n_row, piece, width)
    mixed = [mixed[:, b].reshape(rows, width) for b in range(n_row)]
    mixed = ring4(*mixed, to_row)

    back = dot(act_grads, both, 1, 1).astype(BF).reshape(n_depth, -1, width)
    back = [
        lax.dynamic_index_in_dim(back, (depth + k) % n_depth, 0, keepdims=False)
        for k in range(n_depth)
    ]
    back = ring4(back[0], back[n_depth - 1], back[1], back[2], to_depth)
    back = back.reshape(quarter // piece, n_row, piece, width)
    back = [back[:, b].reshape(quarter, width) for b in range(n_row)]

    share = [
        lax.dynamic_slice_in_dim(mixed, ((depth + k) % n_depth) * quarter, quarter, 0)
        for k in range(n_depth)
    ]
    got = tie(*[to_depth(share[k].astype(BF), k) for k in range(1, n_depth)])
    mixed = share[0]
    for x in got:
        mixed = mixed + x.astype(F32)
    got = tie(*[to_row(back[b].astype(BF), k) for b, k in ((2, 1), (1, -1), (3, 2))])
    back = back[0]
    for x in got:
        back = back + x.astype(F32)
    done = jnp.concatenate([mixed, back], axis=1).astype(BF)
    done = lax.all_gather(done, "depth", axis=0, tiled=True)

    all_tokens = all_tokens.reshape(-1, width)
    all_grads = all_grads.reshape(-1, width)
    grad_down = dot(hidden, all_grads, 0, 0).astype(BF)
    grad_gate = dot(all_tokens, act_grads[:, :hidden_width], 0, 0).astype(BF)
    grad_up = dot(all_tokens, act_grads[:, hidden_width:], 0, 0).astype(BF)
    return (done[:, :width], done[:, width:], grad_gate, grad_up, grad_down)


def solution(mesh):
    in_specs = (
        P("row", "col"),
        P("col", ("row", "depth")),
        P("col", ("row", "depth")),
        P(("row", "depth"), "col"),
        P("row", "col"),
    )
    out_specs = (
        P("row", "col"),
        P("row", "col"),
        P("col", ("row", "depth")),
        P("col", ("row", "depth")),
        P(("row", "depth"), "col"),
    )
    return jax.shard_map(
        per_device, mesh=mesh, in_specs=in_specs, out_specs=out_specs, check_vma=False
    )
```

```python
import jax
import jax.numpy as jnp
from jax import lax
from jax.experimental import pallas as pl
from jax.sharding import PartitionSpec as P

BF = jnp.bfloat16
F32 = jnp.float32
WIRE = jnp.float16
SUM_SCALE = 16.0


def dot(left, right, left_dim, right_dim):
    return lax.dot_general(
        left, right, (((left_dim,), (right_dim,)), ((), ())), preferred_element_type=F32
    )


def tie(*arrays):
    return lax.optimization_barrier(arrays)


def act_gradients(gate_up, grad_hidden, out):
    n = grad_hidden.shape[1]
    gate, up, grad = gate_up[:, :n], gate_up[:, n:], grad_hidden[...]
    sig = jax.nn.sigmoid(gate)
    out[:, :n] = (grad * up * sig * (1.0 + gate * (1.0 - sig))).astype(BF)
    out[:, n:] = (grad * gate * sig).astype(BF)


def per_device(tokens, gate_weight, up_weight, down_weight, grad_out):
    rows, width = tokens.shape
    hidden_width = gate_weight.shape[1]
    n_col = lax.axis_size("col")
    n_row = lax.axis_size("row")
    n_depth = lax.axis_size("depth")
    n_z = n_col // 2
    col = lax.axis_index("col")
    z = col // 2
    core = col % 2
    depth = lax.axis_index("depth")
    half = rows // 2
    piece = rows // n_col
    own_rows = n_row * piece
    far_z = n_z // 2

    def swap(x):
        return lax.ppermute(x, "col", [(i, i ^ 1) for i in range(n_col)])

    def to_z(x, k):
        return lax.ppermute(x, "col", [(i, (i + 2 * k) % n_col) for i in range(n_col)])

    def to_row(x, k):
        return lax.ppermute(x, "row", [(i, (i + k) % n_row) for i in range(n_row)])

    def to_depth(x, k):
        return lax.ppermute(x, "depth", [(i, (i + k) % n_depth) for i in range(n_depth)])

    def gather_rows(x):
        before, after = to_row(x, 1), to_row(x, -1)
        far = jnp.concatenate([to_row(before[:half], 1), to_row(after[half:], -1)], axis=0)
        blocks = [b.reshape(n_col, piece, width) for b in (x, before, after, far)]
        return jnp.concatenate(blocks, axis=1)

    def both_features(x):
        x = x.reshape((n_z, 2) + x.shape[1:])
        mine = lax.dynamic_index_in_dim(x, core, 1, keepdims=False)
        other = lax.dynamic_index_in_dim(x, 1 - core, 1, keepdims=False)
        return mine.reshape(-1, width), swap(other).reshape(-1, width)

    all_tokens = gather_rows(tokens)
    all_grads = gather_rows(grad_out)
    both = jnp.concatenate([gate_weight, up_weight], axis=1)
    both_sib = jnp.concatenate([swap(gate_weight), swap(up_weight)], axis=1)
    down_sib = swap(down_weight)
    t_mine, t_sib = both_features(all_tokens)
    g_mine, g_sib = both_features(all_grads)
    gate_up = (dot(t_mine, both, 1, 0) + dot(t_sib, both_sib, 1, 0)) * SUM_SCALE
    grad_hid = (dot(g_mine, down_weight, 1, 1) + dot(g_sib, down_sib, 1, 1)) * SUM_SCALE

    def ring_sum(parts, beside=()):
        n = parts.shape[1]
        parts = parts.reshape(n_z, own_rows, n)
        cut = (n // 256) * 128

        def part(k):
            return lax.dynamic_index_in_dim(parts, (z + k) % n_z, 0, keepdims=False)

        first = part(far_z).astype(WIRE)
        plus, minus = tie(first[:, :cut], first[:, cut:])
        plus, minus = tie(to_z(plus, 1), to_z(minus, -1))
        plus = jnp.pad(plus.astype(F32), ((0, 0), (0, n - cut)))
        minus = jnp.pad(minus.astype(F32), ((0, 0), (cut, 0)))
        for k in range(far_z - 1, 0, -1):
            plus, minus = (part(k) + plus).astype(WIRE), (part(n_z - k) + minus).astype(WIRE)
            plus, minus, *_ = tie(plus, minus, *(beside if k == far_z - 1 else ()))
            plus, minus = tie(to_z(plus, 1), to_z(minus, -1))
            plus, minus = plus.astype(F32), minus.astype(F32)
        return (part(0) + plus + minus) * (1.0 / SUM_SCALE)

    def both_ways(x):
        return tie(to_z(x, 1), to_z(x, -1))

    def gather(x, plus, minus):
        n = x.shape[1]
        cut = (n // 256) * 128
        out = jnp.zeros((n_z, own_rows, n), x.dtype)

        def put(out, x, k, at=0):
            return lax.dynamic_update_slice(out, x[None], ((z + k) % n_z, 0, at))

        out = put(out, x, 0)
        for k in range(1, far_z):
            if k > 1:
                plus, minus = tie(to_z(plus, 1), to_z(minus, -1))
            out = put(put(out, plus, n_z - k), minus, k)
        plus, minus = tie(to_z(plus[:, :cut], 1), to_z(minus[:, cut:], -1))
        out = put(put(out, plus, far_z), minus, far_z, cut)
        sib = swap(out)
        low, high = jnp.where(core == 0, out, sib), jnp.where(core == 0, sib, out)
        return jnp.stack([low, high], axis=1).reshape(-1, n)

    gate_up = ring_sum(gate_up, (grad_hid,))
    gate, up = gate_up[:, :hidden_width], gate_up[:, hidden_width:]
    hidden = (gate * jax.nn.sigmoid(gate) * up).astype(BF)
    hidden_next = both_ways(hidden)
    grad_hidden = ring_sum(grad_hid)
    hidden = gather(hidden, *hidden_next)
    act_grads = pl.pallas_call(
        act_gradients,
        out_shape=jax.ShapeDtypeStruct((own_rows, 2 * hidden_width), BF),
    )(gate_up, grad_hidden)
    act_grads = lax.all_gather(act_grads, "col", axis=0, tiled=True)

    mid = n_col // 2
    quarter = rows // n_depth

    def ring4(own, last, after, far, move, beside=()):
        cut = far.shape[0] // 2
        low, high = tie(move(far[:cut], 1), move(far[cut:], -1))
        after = jnp.concatenate(
            [(after[:cut].astype(F32) + low.astype(F32)).astype(BF), after[cut:]], axis=0
        )
        last = jnp.concatenate(
            [last[:cut], (last[cut:].astype(F32) + high.astype(F32)).astype(BF)], axis=0
        )
        after, last, *_ = tie(after, last, *beside)
        low, high = tie(move(after, 1), move(last, -1))
        return own.astype(F32) + low.astype(F32) + high.astype(F32)

    mixed = dot(hidden, down_weight, 1, 0).astype(BF)
    mixed = mixed.reshape(n_col, n_row, piece, width)
    mixed = [mixed[:, b].reshape(rows, width) for b in range(n_row)]
    back = dot(act_grads, both, 1, 1).astype(BF)
    mixed = ring4(*mixed, to_row, (back,))
    back = back.reshape(n_depth, -1, width)
    back = [
        lax.dynamic_index_in_dim(back, (depth + k) % n_depth, 0, keepdims=False)
        for k in range(n_depth)
    ]
    back = ring4(back[0], back[n_depth - 1], back[1], back[2], to_depth)
    back = back.reshape(quarter // piece, n_row, piece, width)
    back = [back[:, b].reshape(quarter, width) for b in range(n_row)]

    share = [
        lax.dynamic_slice_in_dim(mixed, ((depth + k) % n_depth) * quarter, quarter, 0)
        for k in range(n_depth)
    ]
    got = tie(*[to_depth(share[k].astype(BF), k) for k in range(1, n_depth)])
    mixed = share[0]
    for x in got:
        mixed = mixed + x.astype(F32)
    got = tie(*[to_row(back[b].astype(BF), k) for b, k in ((2, 1), (1, -1), (3, 2))])
    back = back[0]
    for x in got:
        back = back + x.astype(F32)
    done = jnp.concatenate([mixed, back], axis=1).astype(BF)
    done = lax.all_gather(done, "depth", axis=0, tiled=True)

    all_tokens = all_tokens.reshape(-1, width)
    all_grads = all_grads.reshape(-1, width)
    grad_down = dot(hidden, all_grads, 0, 0).astype(BF)
    grad_gate = dot(all_tokens, act_grads[:, :hidden_width], 0, 0).astype(BF)
    grad_up = dot(all_tokens, act_grads[:, hidden_width:], 0, 0).astype(BF)
    return (done[:, :width], done[:, width:], grad_gate, grad_up, grad_down)


def solution(mesh):
    in_specs = (
        P("row", "col"),
        P("col", ("row", "depth")),
        P("col", ("row", "depth")),
        P(("row", "depth"), "col"),
        P("row", "col"),
    )
    out_specs = (
        P("row", "col"),
        P("row", "col"),
        P("col", ("row", "depth")),
        P("col", ("row", "depth")),
        P(("row", "depth"), "col"),
    )
    return jax.shard_map(
        per_device, mesh=mesh, in_specs=in_specs, out_specs=out_specs, check_vma=False
    )
```

```python
import jax
import jax.numpy as jnp
from jax import lax
from jax.experimental import pallas as pl
from jax.sharding import PartitionSpec as P

BF = jnp.bfloat16
F32 = jnp.float32
WIRE = jnp.float16
SUM_SCALE = 2.0**20


def dot(left, right, left_dim, right_dim):
    return lax.dot_general(
        left, right, (((left_dim,), (right_dim,)), ((), ())), preferred_element_type=F32
    )


def pack(x):
    return (x * lax.rsqrt(jnp.maximum(jnp.abs(x), 1e-30))).astype(WIRE)


def unpack(x):
    x = x.astype(F32)
    return x * jnp.abs(x)


def tie(*arrays):
    return lax.optimization_barrier(arrays)


def act_gradients(gate_up, grad_hidden, out):
    n = grad_hidden.shape[1]
    gate, up, grad = gate_up[:, :n], gate_up[:, n:], grad_hidden[...]
    sig = jax.nn.sigmoid(gate)
    out[:, :n] = (grad * up * sig * (1.0 + gate * (1.0 - sig))).astype(BF)
    out[:, n:] = (grad * gate * sig).astype(BF)


def per_device(tokens, gate_weight, up_weight, down_weight, grad_out):
    rows, width = tokens.shape
    hidden_width = gate_weight.shape[1]
    n_col = lax.axis_size("col")
    n_row = lax.axis_size("row")
    n_depth = lax.axis_size("depth")
    n_z = n_col // 2
    col = lax.axis_index("col")
    z = col // 2
    core = col % 2
    depth = lax.axis_index("depth")
    half = rows // 2
    piece = rows // n_col
    own_rows = n_row * piece
    far_z = n_z // 2

    def swap(x):
        return lax.ppermute(x, "col", [(i, i ^ 1) for i in range(n_col)])

    def to_z(x, k):
        return lax.ppermute(x, "col", [(i, (i + 2 * k) % n_col) for i in range(n_col)])

    def to_row(x, k):
        return lax.ppermute(x, "row", [(i, (i + k) % n_row) for i in range(n_row)])

    def to_depth(x, k):
        return lax.ppermute(x, "depth", [(i, (i + k) % n_depth) for i in range(n_depth)])

    def gather_rows(x):
        before, after = to_row(x, 1), to_row(x, -1)
        far = jnp.concatenate([to_row(before[:half], 1), to_row(after[half:], -1)], axis=0)
        blocks = [b.reshape(n_col, piece, width) for b in (x, before, after, far)]
        return jnp.concatenate(blocks, axis=1)

    def both_features(x):
        x = x.reshape((n_z, 2) + x.shape[1:])
        mine = lax.dynamic_index_in_dim(x, core, 1, keepdims=False)
        other = lax.dynamic_index_in_dim(x, 1 - core, 1, keepdims=False)
        return mine.reshape(-1, width), swap(other).reshape(-1, width)

    all_tokens = gather_rows(tokens)
    all_grads = gather_rows(grad_out)
    both = jnp.concatenate([gate_weight, up_weight], axis=1)
    both_sib = jnp.concatenate([swap(gate_weight), swap(up_weight)], axis=1)
    down_sib = swap(down_weight)
    t_mine, t_sib = both_features(all_tokens)
    g_mine, g_sib = both_features(all_grads)
    gate_up = (dot(t_mine, both, 1, 0) + dot(t_sib, both_sib, 1, 0)) * SUM_SCALE
    grad_hid = (dot(g_mine, down_weight, 1, 1) + dot(g_sib, down_sib, 1, 1)) * SUM_SCALE

    def ring_sum(parts, beside=()):
        n = parts.shape[1]
        parts = parts.reshape(n_z, own_rows, n)
        cut = (n // 256) * 128

        def part(k):
            return lax.dynamic_index_in_dim(parts, (z + k) % n_z, 0, keepdims=False)

        first = pack(part(far_z))
        plus, minus = tie(first[:, :cut], first[:, cut:])
        plus, minus = tie(to_z(plus, 1), to_z(minus, -1))
        plus = jnp.pad(plus, ((0, 0), (0, n - cut)))
        minus = jnp.pad(minus, ((0, 0), (cut, 0)))
        for k in range(far_z - 1, 0, -1):
            plus, minus = pack(part(k) + unpack(plus)), pack(part(n_z - k) + unpack(minus))
            plus, minus, *_ = tie(plus, minus, *(beside if k == far_z - 1 else ()))
            plus, minus = tie(to_z(plus, 1), to_z(minus, -1))
        return (part(0) + unpack(plus) + unpack(minus)) * (1.0 / SUM_SCALE)

    def both_ways(x):
        return tie(to_z(x, 1), to_z(x, -1))

    def gather(x, plus, minus):
        n = x.shape[1]
        cut = (n // 256) * 128
        out = jnp.zeros((n_z, own_rows, n), x.dtype)

        def put(out, x, k, at=0):
            return lax.dynamic_update_slice(out, x[None], ((z + k) % n_z, 0, at))

        out = put(out, x, 0)
        for k in range(1, far_z):
            if k > 1:
                plus, minus = tie(to_z(plus, 1), to_z(minus, -1))
            out = put(put(out, plus, n_z - k), minus, k)
        plus, minus = tie(to_z(plus[:, :cut], 1), to_z(minus[:, cut:], -1))
        out = put(put(out, plus, far_z), minus, far_z, cut)
        sib = swap(out)
        low, high = jnp.where(core == 0, out, sib), jnp.where(core == 0, sib, out)
        return jnp.stack([low, high], axis=1).reshape(-1, n)

    gate_up = ring_sum(gate_up, (grad_hid,))
    gate, up = gate_up[:, :hidden_width], gate_up[:, hidden_width:]
    hidden = (gate * jax.nn.sigmoid(gate) * up).astype(BF)
    hidden_next = both_ways(hidden)
    grad_hidden = ring_sum(grad_hid)
    hidden = gather(hidden, *hidden_next)
    act_grads = pl.pallas_call(
        act_gradients,
        out_shape=jax.ShapeDtypeStruct((own_rows, 2 * hidden_width), BF),
    )(gate_up, grad_hidden)
    act_grads = lax.all_gather(act_grads, "col", axis=0, tiled=True)

    mid = n_col // 2
    quarter = rows // n_depth

    def ring4(own, last, after, far, move, beside=()):
        cut = far.shape[0] // 2
        low, high = tie(move(far[:cut], 1), move(far[cut:], -1))
        after = jnp.concatenate(
            [(after[:cut].astype(F32) + low.astype(F32)).astype(BF), after[cut:]], axis=0
        )
        last = jnp.concatenate(
            [last[:cut], (last[cut:].astype(F32) + high.astype(F32)).astype(BF)], axis=0
        )
        after, last, *_ = tie(after, last, *beside)
        low, high = tie(move(after, 1), move(last, -1))
        return own.astype(F32) + low.astype(F32) + high.astype(F32), after

    mixed = dot(hidden, down_weight, 1, 0).astype(BF)
    mixed = mixed.reshape(n_col, n_row, piece, width)
    mixed = [mixed[:, b].reshape(rows, width) for b in range(n_row)]
    back = dot(act_grads, both, 1, 1).astype(BF)
    all_grads, _ = tie(all_grads, back)
    mixed, _ = ring4(*mixed, to_row, (back,))
    back = back.reshape(n_depth, -1, width)
    back = [
        lax.dynamic_index_in_dim(back, (depth + k) % n_depth, 0, keepdims=False)
        for k in range(n_depth)
    ]
    back, sent = ring4(back[0], back[n_depth - 1], back[1], back[2], to_depth)
    all_tokens, _ = tie(all_tokens, sent)
    back = back.reshape(quarter // piece, n_row, piece, width)
    back = [back[:, b].reshape(quarter, width) for b in range(n_row)]

    share = [
        lax.dynamic_slice_in_dim(mixed, ((depth + k) % n_depth) * quarter, quarter, 0)
        for k in range(n_depth)
    ]
    sends = [(x.astype(BF), to_row, k) for x, k in ((back[2], 1), (back[1], -1), (back[3], 2))]
    sends += [(share[k].astype(BF), to_depth, k) for k in range(1, n_depth)]
    ready = tie(*[x for x, _, _ in sends])
    got = tie(*[move(x, k) for x, (_, move, k) in zip(ready, sends)])
    back, mixed = back[0], share[0]
    for x in got[: n_row - 1]:
        back = back + x.astype(F32)
    for x in got[n_row - 1 :]:
        mixed = mixed + x.astype(F32)
    done = jnp.concatenate([mixed, back], axis=1).astype(BF)
    done = lax.all_gather(done, "depth", axis=0, tiled=True)

    all_tokens = all_tokens.reshape(-1, width)
    all_grads = all_grads.reshape(-1, width)
    grad_down = dot(hidden, all_grads, 0, 0).astype(BF)
    grad_gate = dot(all_tokens, act_grads[:, :hidden_width], 0, 0).astype(BF)
    grad_up = dot(all_tokens, act_grads[:, hidden_width:], 0, 0).astype(BF)
    return (done[:, :width], done[:, width:], grad_gate, grad_up, grad_down)


def solution(mesh):
    in_specs = (
        P("row", "col"),
        P("col", ("row", "depth")),
        P("col", ("row", "depth")),
        P(("row", "depth"), "col"),
        P("row", "col"),
    )
    out_specs = (
        P("row", "col"),
        P("row", "col"),
        P("col", ("row", "depth")),
        P("col", ("row", "depth")),
        P(("row", "depth"), "col"),
    )
    return jax.shard_map(
        per_device, mesh=mesh, in_specs=in_specs, out_specs=out_specs, check_vma=False
    )
```

```python
import jax
import jax.numpy as jnp
from jax import lax
from jax.experimental import pallas as pl
from jax.sharding import PartitionSpec as P

BF = jnp.bfloat16
F32 = jnp.float32
WIRE = jnp.float16
SUM_SCALE = 2.0**20


def dot(left, right, left_dim, right_dim):
    return lax.dot_general(
        left, right, (((left_dim,), (right_dim,)), ((), ())), preferred_element_type=F32
    )


def pack(x):
    return (x * lax.rsqrt(jnp.maximum(jnp.abs(x), 1e-30))).astype(WIRE)


def unpack(x):
    x = x.astype(F32)
    return x * jnp.abs(x)


def tie(*arrays):
    return lax.optimization_barrier(arrays)


def act_gradients(gate_up, grad_hidden, out):
    n = grad_hidden.shape[1]
    gate, up, grad = gate_up[:, :n], gate_up[:, n:], grad_hidden[...]
    sig = jax.nn.sigmoid(gate)
    out[:, :n] = (grad * up * sig * (1.0 + gate * (1.0 - sig))).astype(BF)
    out[:, n:] = (grad * gate * sig).astype(BF)


def per_device(tokens, gate_weight, up_weight, down_weight, grad_out):
    rows, width = tokens.shape
    hidden_width = gate_weight.shape[1]
    n_col = lax.axis_size("col")
    n_row = lax.axis_size("row")
    n_depth = lax.axis_size("depth")
    n_z = n_col // 2
    col = lax.axis_index("col")
    z = col // 2
    core = col % 2
    depth = lax.axis_index("depth")
    half = rows // 2
    piece = rows // n_col
    own_rows = n_row * piece
    far_z = n_z // 2

    def swap(x):
        return lax.ppermute(x, "col", [(i, i ^ 1) for i in range(n_col)])

    def to_z(x, k):
        return lax.ppermute(x, "col", [(i, (i + 2 * k) % n_col) for i in range(n_col)])

    def to_row(x, k):
        return lax.ppermute(x, "row", [(i, (i + k) % n_row) for i in range(n_row)])

    def to_depth(x, k):
        return lax.ppermute(x, "depth", [(i, (i + k) % n_depth) for i in range(n_depth)])

    def gather_rows(x):
        before, after = to_row(x, 1), to_row(x, -1)
        far = jnp.concatenate([to_row(before[:half], 1), to_row(after[half:], -1)], axis=0)
        blocks = [b.reshape(n_col, piece, width) for b in (x, before, after, far)]
        return jnp.concatenate(blocks, axis=1)

    def both_features(x):
        x = x.reshape((n_z, 2) + x.shape[1:])
        mine = lax.dynamic_index_in_dim(x, core, 1, keepdims=False)
        other = lax.dynamic_index_in_dim(x, 1 - core, 1, keepdims=False)
        return mine.reshape(-1, width), swap(other).reshape(-1, width)

    all_tokens = gather_rows(tokens)
    all_grads = gather_rows(grad_out)
    both = jnp.concatenate([gate_weight, up_weight], axis=1)
    both_sib = jnp.concatenate([swap(gate_weight), swap(up_weight)], axis=1)
    down_sib = swap(down_weight)
    t_mine, t_sib = both_features(all_tokens)
    g_mine, g_sib = both_features(all_grads)
    gate_up = (dot(t_mine, both, 1, 0) + dot(t_sib, both_sib, 1, 0)) * SUM_SCALE
    grad_hid = (dot(g_mine, down_weight, 1, 1) + dot(g_sib, down_sib, 1, 1)) * SUM_SCALE

    def ring_sum(parts, beside=()):
        n = parts.shape[1]
        parts = parts.reshape(n_z, own_rows, n)
        cut = (n // 256) * 128

        def part(k):
            return lax.dynamic_index_in_dim(parts, (z + k) % n_z, 0, keepdims=False)

        first = pack(part(far_z))
        plus, minus = tie(first[:, :cut], first[:, cut:])
        plus, minus = tie(to_z(plus, 1), to_z(minus, -1))
        plus = jnp.pad(plus, ((0, 0), (0, n - cut)))
        minus = jnp.pad(minus, ((0, 0), (cut, 0)))
        for k in range(far_z - 1, 0, -1):
            plus, minus = pack(part(k) + unpack(plus)), pack(part(n_z - k) + unpack(minus))
            plus, minus, *_ = tie(plus, minus, *(beside if k == far_z - 1 else ()))
            plus, minus = tie(to_z(plus, 1), to_z(minus, -1))
        return (part(0) + unpack(plus) + unpack(minus)) * (1.0 / SUM_SCALE)

    def both_ways(x):
        return tie(to_z(x, 1), to_z(x, -1))

    def gather(x, plus, minus):
        n = x.shape[1]
        cut = (n // 256) * 128
        out = jnp.zeros((n_z, own_rows, n), x.dtype)

        def put(out, x, k, at=0):
            return lax.dynamic_update_slice(out, x[None], ((z + k) % n_z, 0, at))

        out = put(out, x, 0)
        for k in range(1, far_z):
            if k > 1:
                plus, minus = tie(to_z(plus, 1), to_z(minus, -1))
            out = put(put(out, plus, n_z - k), minus, k)
        plus, minus = tie(to_z(plus[:, :cut], 1), to_z(minus[:, cut:], -1))
        out = put(put(out, plus, far_z), minus, far_z, cut)
        sib = swap(out)
        low, high = jnp.where(core == 0, out, sib), jnp.where(core == 0, sib, out)
        return jnp.stack([low, high], axis=1).reshape(-1, n)

    gate_up = ring_sum(gate_up, (grad_hid,))
    gate, up = gate_up[:, :hidden_width], gate_up[:, hidden_width:]
    hidden = (gate * jax.nn.sigmoid(gate) * up).astype(BF)
    hidden_next = both_ways(hidden)
    grad_hidden = ring_sum(grad_hid)
    hidden = gather(hidden, *hidden_next)
    act_grads = pl.pallas_call(
        act_gradients,
        out_shape=jax.ShapeDtypeStruct((own_rows, 2 * hidden_width), BF),
    )(gate_up, grad_hidden)
    act_grads = lax.all_gather(act_grads, "col", axis=0, tiled=True)

    mid = n_col // 2
    quarter = rows // n_depth

    def ring4(own, last, after, far, move, beside=()):
        cut = far.shape[0] // 2
        low, high = tie(move(far[:cut], 1), move(far[cut:], -1))
        after = jnp.concatenate(
            [(after[:cut].astype(F32) + low.astype(F32)).astype(BF), after[cut:]], axis=0
        )
        last = jnp.concatenate(
            [last[:cut], (last[cut:].astype(F32) + high.astype(F32)).astype(BF)], axis=0
        )
        after, last, *_ = tie(after, last, *beside)
        low, high = tie(move(after, 1), move(last, -1))
        return own.astype(F32) + low.astype(F32) + high.astype(F32)

    mixed = dot(hidden, down_weight, 1, 0).astype(BF)
    mixed = mixed.reshape(n_col, n_row, piece, width)
    mixed = [mixed[:, b].reshape(rows, width) for b in range(n_row)]
    back = dot(act_grads, both, 1, 1).astype(BF)
    mixed = ring4(*mixed, to_row, (back,))
    back = back.reshape(n_depth, -1, width)
    back = [
        lax.dynamic_index_in_dim(back, (depth + k) % n_depth, 0, keepdims=False)
        for k in range(n_depth)
    ]
    back = ring4(back[0], back[n_depth - 1], back[1], back[2], to_depth)
    back = back.reshape(quarter // piece, n_row, piece, width)
    back = [back[:, b].reshape(quarter, width) for b in range(n_row)]

    share = [
        lax.dynamic_slice_in_dim(mixed, ((depth + k) % n_depth) * quarter, quarter, 0)
        for k in range(n_depth)
    ]
    got = tie(*[to_depth(share[k].astype(BF), k) for k in range(1, n_depth)])
    mixed = share[0]
    for x in got:
        mixed = mixed + x.astype(F32)
    got = tie(*[to_row(back[b].astype(BF), k) for b, k in ((2, 1), (1, -1), (3, 2))])
    back = back[0]
    for x in got:
        back = back + x.astype(F32)
    done = jnp.concatenate([mixed, back], axis=1).astype(BF)
    done = lax.all_gather(done, "depth", axis=0, tiled=True)

    all_tokens = all_tokens.reshape(-1, width)
    all_grads = all_grads.reshape(-1, width)
    grad_down = dot(hidden, all_grads, 0, 0).astype(BF)
    grad_gate = dot(all_tokens, act_grads[:, :hidden_width], 0, 0).astype(BF)
    grad_up = dot(all_tokens, act_grads[:, hidden_width:], 0, 0).astype(BF)
    return (done[:, :width], done[:, width:], grad_gate, grad_up, grad_down)


def solution(mesh):
    in_specs = (
        P("row", "col"),
        P("col", ("row", "depth")),
        P("col", ("row", "depth")),
        P(("row", "depth"), "col"),
        P("row", "col"),
    )
    out_specs = (
        P("row", "col"),
        P("row", "col"),
        P("col", ("row", "depth")),
        P("col", ("row", "depth")),
        P(("row", "depth"), "col"),
    )
    return jax.shard_map(
        per_device, mesh=mesh, in_specs=in_specs, out_specs=out_specs, check_vma=False
    )
```
